32 devices in a mesh: parts: 2 (over x), row: 16 (over z, y, core).
Axes of the slice: x: 2, y: 2, z: 4, core: 2. Of those that a mesh axis runs over, the one named last changes fastest.
Arguments:
- vectors: bfloat16 [32768, 128], P(('parts', 'row')), parts along dimension 0, may hold values from -6 to 6
- tiles: bfloat16 [8192, 128, 128], P(('parts', 'row')), parts along dimension 0, may hold values from -0.046875 to 0.046875
- tile_cols: int32 [8192], P(('parts', 'row')), parts along dimension 0, may hold values from -1 to 127, as said below
- ritz: bfloat16 [256, 128], P('parts'), parts along dimension 0, may hold values from -0.5 to 0.5
Outputs:
- rotated: bfloat16 [32768, 128], P(('parts', 'row')), parts along dimension 0
- gram: float32 [256, 128], P('parts'), parts along dimension 0
The draws below stay inside these ranges and needn't reach their ends.
There are 2 independent parts, one for each index of `parts`. The reference program is written for one: setup_inputs(seed, part) draws one part's arguments, and reference() takes and returns one part's arrays. A program takes and returns all parts, laid end to end along the dimension named above; each array names one. Nothing has to cross between parts.
Inputs may be any that keep to these rules, and one draw needn't show every extreme that they name: `tile_cols`: entry t * 32 + j belongs to tile row t; the live slots of a tile row come first and the rest are -1; every tile row has 8 or more live slots and some tile row has all 32; a live column lies between (t // 8 - 2) * 8 and (t // 8 + 3) * 8 - 1.
All inputs are finite; a program needn't handle non-finite values.
Results may differ from the reference program's by a relative error of at most 0.0058.
Values may be sent and summed in bfloat16 or wider, within the bound.
A program may use at most 64 MiB of HBM per device.

```python
import jax
import jax.numpy as jnp
from jax import lax

TILE = 128
NVEC = 128
TR = 8
TILES_ROW = 32
REACH = 2
DEG = 4
TROWS = 128
NODES = 16384
SLOTS = 4096


def draw_tile_cols(key, part):
    key = jax.random.fold_in(key, 7)
    key_count, key_full, key_cols = jax.random.split(key, 3)
    counts = jax.random.randint(key_count, (TROWS,), TILES_ROW // 4, TILES_ROW + 1)
    full_row = jax.random.randint(key_full, (), 0, TROWS)
    counts = jnp.where(jnp.arange(TROWS) == full_row, TILES_ROW, counts)
    owner = jnp.arange(TROWS) // TR
    lowest = jnp.maximum(owner - REACH, 0) * TR
    highest = jnp.minimum(owner + REACH + 1, TROWS // TR) * TR
    columns = jax.random.randint(key_cols, (TROWS, TILES_ROW), lowest[:, None], highest[:, None])
    slot_pos = jnp.arange(TILES_ROW)[None, :]
    return jnp.where(slot_pos < counts[:, None], columns, -1).reshape(-1).astype(jnp.int32)


def levels(stream_key, dims, cuts, smallest, top_value):
    def one(dim, shards_of):
        steps = jax.random.uniform(jax.random.fold_in(jax.random.fold_in(stream_key, 6), dim), (shards_of,), jnp.float32, smallest / len(cuts), top_value / len(cuts))
        return jnp.repeat(jnp.exp(steps), dims[dim] // shards_of).reshape((-1,) + (1,) * (len(dims) - dim - 1))

    factor_of = one(*cuts[0])
    for cut in cuts[1:]:
        factor_of = factor_of * one(*cut)
    return factor_of


def scatter_about(key, extent, spread, most, cuts=(), kind=jnp.bfloat16):
    array = spread * jax.random.normal(key, extent, jnp.float32)
    if cuts:
        array = array * levels(key, extent, cuts, -0.22, 0.18)
    return jnp.clip(array, -most, most).astype(kind)


def setup_inputs(seed: int = 0, part: int = 0) -> dict:
    splits = jax.random.split(jax.random.key(seed), 5)
    own_keys = jax.random.split(jax.random.fold_in(splits[4], part), 5)
    vectors = scatter_about(own_keys[0], (NODES, NVEC), 1.0, 6.0, ((0, 16),))
    tiles = scatter_about(own_keys[1], (SLOTS, TILE, TILE), (4 * TILE * TILES_ROW) ** -0.5, 0.046875, ((0, 16),))
    tile_cols = draw_tile_cols(jax.random.fold_in(jax.random.fold_in(splits[4], part), 71), part)
    ritz = scatter_about(own_keys[3], (NVEC, NVEC), NVEC ** -0.5, 0.5)
    return dict(vectors=vectors, tiles=tiles, tile_cols=tile_cols, ritz=ritz)


def apply_operator(current, tiles, tile_cols):
    blocks = current.reshape(TROWS, TILE, NVEC)
    grouped = tiles.reshape(TROWS, TILES_ROW, TILE, TILE)
    columns = tile_cols.reshape(TROWS, TILES_ROW)

    def one_row(pair):
        row_tiles, cols = pair
        picked = blocks[jnp.maximum(cols, 0).astype(jnp.int32)]
        picked = jnp.where((cols >= 0)[:, None, None], picked, jnp.zeros_like(picked))
        return jnp.einsum("jab,jbk->ak", row_tiles.astype(jnp.float32), picked.astype(jnp.float32))

    return lax.map(one_row, (grouped, columns)).reshape(NODES, NVEC)


def reference(vectors, tiles, tile_cols, ritz):
    previous = vectors
    current = apply_operator(vectors, tiles, tile_cols).astype(jnp.bfloat16)
    for step in range(DEG - 1):
        nxt = 2.0 * apply_operator(current, tiles, tile_cols) - previous.astype(jnp.float32)
        previous, current = current, nxt.astype(jnp.bfloat16)
    wide = current.astype(jnp.float32)
    gram = jnp.einsum("nk,nl->kl", wide, wide) * (float(NODES) ** -0.5)
    rotated = jnp.dot(current, ritz, preferred_element_type=jnp.float32).astype(jnp.bfloat16)
    return rotated, gram
```

```python
import functools

import jax
import jax.numpy as jnp
from jax import lax
from jax.experimental import pallas as pl
from jax.experimental.pallas import tpu as pltpu
from jax.sharding import PartitionSpec as P

REACH = 2
DEG = 4
CHUNK = 1
OWN, SIB, PAR, OTH, EXT = range(5)


def kernel(nrow, per_row, vec, tiles_hbm, cols, ritz, rot, gram, e0, e1, e2, e3, tiles, pos, fil, part, rs, tot, gath,
           tile_sem, own_sem, send_sem, recv_sem, g_send, g_recv, a_send, a_recv):
    ext = (e0, e1, e2, e3)
    tr, tile, width = vec.shape
    nch = tr // CHUNK
    zero_block = 5 * tr
    me = lax.axis_index("row")
    core = lax.rem(me, 2)
    chip = lax.div(me, 2)
    odd = lax.rem(chip, 2)
    sign = 1 - 2 * odd
    near = 1 - odd
    is_near = core == near
    sib = me + 1 - 2 * core
    partner = me + 2 * sign
    ahead = me + 4 * sign
    behind = me - 4 * sign
    has_ahead = jnp.logical_and(ahead >= 0, ahead < nrow)
    has_behind = jnp.logical_and(behind >= 0, behind < nrow)

    own_copy = pltpu.make_async_copy(vec, e0.at[pl.ds(0, tr)], own_sem)
    own_copy.start()

    def tile_copy(t):
        rows = pl.ds(t * per_row, per_row)
        return pltpu.make_async_copy(tiles_hbm.at[rows], tiles.at[rows], tile_sem.at[t])

    barrier = pltpu.get_barrier_semaphore()

    def greet(d, _):
        pl.semaphore_signal(barrier, inc=1, device_id={"row": lax.rem(me + d, nrow)}, device_id_type=pl.DeviceIdType.MESH)
        return 0

    lax.fori_loop(1, nrow, greet, 0)
    pl.semaphore_wait(barrier, nrow - 1)

    def send(k, kind, ch, src=None):
        buf = ext[k]
        at = ch * CHUNK
        origin, place, target = (
            (OWN, SIB, sib),
            (OWN, PAR, partner),
            (PAR, OTH, ahead),
            (PAR + is_near.astype(jnp.int32), EXT, sib),
        )[kind]
        source = buf.at[pl.ds(origin * tr + at, CHUNK)] if src is None else src.at[pl.ds(at, CHUNK)]
        return pltpu.make_async_remote_copy(
            src_ref=source,
            dst_ref=buf.at[pl.ds(place * tr + at, CHUNK)],
            send_sem=send_sem.at[k, kind, ch],
            recv_sem=recv_sem.at[k, kind, ch],
            device_id={"row": target},
            device_id_type=pl.DeviceIdType.MESH,
        )

    def send_own(k, ch, src=None):
        send(k, 1, ch, src).start()
        send(k, 0, ch, src).start()

    def forward_partner(k, ch):
        send(k, 1, ch).wait_recv()

        @pl.when(has_ahead)
        def _():
            send(k, 2, ch).start()

        @pl.when(jnp.logical_not(is_near))
        def _():
            send(k, 3, ch).start()

    def forward_other(k, ch):
        @pl.when(has_behind)
        def _():
            send(k, 2, ch).wait_recv()

            @pl.when(is_near)
            def _():
                send(k, 3, ch).start()

    def forward_all(k):
        forward_partner(k, 0)

        def one(ch, _):
            forward_partner(k, ch)
            forward_other(k, ch - 1)
            return 0

        lax.fori_loop(1, nch, one, 0)
        forward_other(k, nch - 1)

        def rest(ch, _):
            send(k, 0, ch).wait_recv()

            @pl.when(jnp.logical_or(is_near, has_behind))
            def _():
                send(k, 3, ch).wait_recv()

            return 0

        lax.fori_loop(0, nch, rest, 0)

    for ch in range(nch):
        send_own(0, ch, vec)
    for t in range(tr):
        tile_copy(t).start()
    for buf in ext:
        buf[zero_block] = jnp.zeros((tile, width), buf.dtype)

    first_col = (me - REACH) * tr

    def place_of(i, _):
        col = cols[i]
        rel = jnp.where(col >= 0, col - first_col, 0)
        owner = me - REACH + lax.div(rel, tr)
        slot = jnp.where(
            owner == me, OWN,
            jnp.where(owner == sib, SIB, jnp.where(owner == partner, PAR, jnp.where(owner == me - 2 * sign, OTH, EXT))),
        )
        pos[i] = jnp.where(col >= 0, slot * tr + lax.rem(rel, tr), zero_block)
        return 0

    lax.fori_loop(0, tr * per_row, place_of, 0)

    own_copy.wait()
    part[...] = jnp.zeros_like(part)
    for k in range(DEG):
        forward_all(k)
        buf = ext[k]

        def one_row(t, _):
            if k == 0:
                tile_copy(t).wait()
            lhs = jnp.concatenate([tiles[t * per_row + j] for j in range(per_row)], axis=1)
            rhs = jnp.concatenate([buf[pos[t * per_row + j]] for j in range(per_row)], axis=0)
            acc = jnp.dot(lhs, rhs, preferred_element_type=jnp.float32)
            if k > 0:
                acc = 2.0 * acc - ext[k - 1][t].astype(jnp.float32)
            y = acc.astype(jnp.bfloat16)
            if k < DEG - 1:
                ext[k + 1][t] = y
                if CHUNK == 1:
                    send_own(k + 1, t)
                else:
                    @pl.when(lax.rem(t, CHUNK) == CHUNK - 1)
                    def _():
                        send_own(k + 1, lax.div(t, CHUNK))
            else:
                fil[t] = y
                part[...] += lax.dot_general(y, y, (((0,), (0,)), ((), ())), preferred_element_type=jnp.float32).reshape(part.shape)
            return 0

        lax.fori_loop(0, tr, one_row, 0)

    def scatter(d):
        target = lax.rem(me + d, nrow)
        return pltpu.make_async_remote_copy(
            src_ref=part.at[target], dst_ref=rs.at[d], send_sem=g_send.at[d], recv_sem=g_recv.at[d],
            device_id={"row": target}, device_id_type=pl.DeviceIdType.MESH)

    def spread(d):
        target = lax.rem(me + d, nrow)
        return pltpu.make_async_remote_copy(
            src_ref=tot, dst_ref=gath.at[me], send_sem=a_send.at[d], recv_sem=a_recv.at[d],
            device_id={"row": target}, device_id_type=pl.DeviceIdType.MESH)

    for d in range(1, nrow):
        scatter(d).start()

    def rotate(t, _):
        rot[t] = jnp.dot(fil[t], ritz[...], preferred_element_type=jnp.float32).astype(rot.dtype)
        return 0

    lax.fori_loop(0, tr, rotate, 0)
    total = part[me]
    for d in range(1, nrow):
        scatter(d).wait_recv()
        total = total + rs[d]
    total = total * float(nrow * tr * tile) ** (-0.5)
    tot[...] = total
    for d in range(1, nrow):
        spread(d).start()
    gath[me] = total
    for k in range(DEG):
        def drain(ch, _):
            send(k, 0, ch).wait_send()
            send(k, 1, ch).wait_send()

            @pl.when(has_ahead)
            def _():
                send(k, 2, ch).wait_send()

            @pl.when(jnp.logical_or(jnp.logical_not(is_near), has_behind))
            def _():
                send(k, 3, ch).wait_send()

            return 0

        lax.fori_loop(0, nch, drain, 0)
    for d in range(1, nrow):
        scatter(d).wait_send()
    for d in range(1, nrow):
        spread(d).wait_recv()
        spread(d).wait_send()
    gram[...] = gath[...]


def body(vectors, tiles, tile_cols, ritz):
    rows_here, width = vectors.shape
    tile = tiles.shape[1]
    tr = rows_here // tile
    per_row = tiles.shape[0] // tr
    nrow = lax.axis_size("row")
    nch = tr // CHUNK
    share = (nrow, width // nrow, width)
    vmem = pl.BlockSpec(memory_space=pltpu.VMEM)
    ext = pltpu.VMEM((5 * tr + 1, tile, width), jnp.bfloat16)
    rot, gram = pl.pallas_call(
        functools.partial(kernel, nrow, per_row),
        out_shape=(
            jax.ShapeDtypeStruct((tr, tile, width), jnp.bfloat16),
            jax.ShapeDtypeStruct(share, jnp.float32),
        ),
        in_specs=[
            pl.BlockSpec(memory_space=pl.ANY),
            pl.BlockSpec(memory_space=pl.ANY),
            pl.BlockSpec(memory_space=pltpu.SMEM),
            vmem,
        ],
        out_specs=(vmem, vmem),
        scratch_shapes=[
            ext, ext, ext, ext,
            pltpu.VMEM(tiles.shape, jnp.bfloat16),
            pltpu.SMEM((tr * per_row,), jnp.int32),
            pltpu.VMEM((tr, tile, width), jnp.bfloat16),
            pltpu.VMEM(share, jnp.float32),
            pltpu.VMEM(share, jnp.float32),
            pltpu.VMEM(share[1:], jnp.float32),
            pltpu.VMEM(share, jnp.float32),
            pltpu.SemaphoreType.DMA((tr,)),
            pltpu.SemaphoreType.DMA,
            pltpu.SemaphoreType.DMA((DEG, 4, nch)),
            pltpu.SemaphoreType.DMA((DEG, 4, nch)),
            pltpu.SemaphoreType.DMA((nrow,)),
            pltpu.SemaphoreType.DMA((nrow,)),
            pltpu.SemaphoreType.DMA((nrow,)),
            pltpu.SemaphoreType.DMA((nrow,)),
        ],
        compiler_params=pltpu.CompilerParams(
            collective_id=0, has_side_effects=True, vmem_limit_bytes=56 * 2**20
        ),
        cost_estimate=pl.CostEstimate(
            flops=2 * DEG * tiles.size * width, bytes_accessed=2 * tiles.size, transcendentals=0
        ),
    )(vectors.reshape(tr, tile, width), tiles, tile_cols, ritz)
    return rot.reshape(rows_here, width), gram.reshape(width, width)


def solution(mesh):
    return jax.shard_map(
        body,
        mesh=mesh,
        in_specs=(
            P(("parts", "row"), None),
            P(("parts", "row"), None, None),
            P(("parts", "row")),
            P("parts", None),
        ),
        out_specs=(P(("parts", "row"), None), P("parts", None)),
        check_vma=False,
    )
```

```python
import functools

import jax
import jax.numpy as jnp
from jax import lax
from jax.experimental import pallas as pl
from jax.experimental.pallas import tpu as pltpu
from jax.sharding import PartitionSpec as P

REACH = 2
DEG = 4
CHUNK = 1
PARTNER_LAG = 4
OTHER_LAG = 8
DIRECT = 1
OWN, SIB, PAR, OTH, EXT = range(5)


def kernel(nrow, per_row, vec, tiles_hbm, cols, ritz, rot, gram, e0, e1, e2, e3, tiles, table, pos, fil, part, rs, tot, gath,
           tile_sem, own_sem, send_sem, recv_sem, g_send, g_recv, a_send, a_recv):
    ext = (e0, e1, e2, e3)
    tr, tile, width = vec.shape
    nch = tr // CHUNK
    zero_block = 5 * tr
    me = lax.axis_index("row")
    core = lax.rem(me, 2)
    chip = lax.div(me, 2)
    odd = lax.rem(chip, 2)
    sign = 1 - 2 * odd
    near = 1 - odd
    is_near = core == near
    sib = me + 1 - 2 * core
    partner = me + 2 * sign
    ahead = me + 4 * sign
    behind = me - 4 * sign
    far = ahead + 1 - 2 * core
    has_ahead = jnp.logical_and(ahead >= 0, ahead < nrow)
    has_behind = jnp.logical_and(behind >= 0, behind < nrow)

    own_copy = pltpu.make_async_copy(vec, e0.at[pl.ds(0, tr)], own_sem)
    own_copy.start()

    def tile_copy(t):
        rows = pl.ds(t * per_row, per_row)
        return pltpu.make_async_copy(tiles_hbm.at[rows], tiles.at[rows], tile_sem.at[t])

    barrier = pltpu.get_barrier_semaphore()

    def greet(d, _):
        pl.semaphore_signal(barrier, inc=1, device_id={"row": lax.rem(me + d, nrow)}, device_id_type=pl.DeviceIdType.MESH)
        return 0

    lax.fori_loop(1, nrow, greet, 0)
    pl.semaphore_wait(barrier, nrow - 1)

    def send(k, kind, ch, src=None):
        buf = ext[k]
        at = ch * CHUNK
        origin, place, target = (
            (OWN, SIB, sib),
            (OWN, PAR, partner),
            (PAR, OTH, ahead),
            (PAR + is_near.astype(jnp.int32), EXT, sib),
            (PAR, EXT, far),
        )[kind]
        source = buf.at[pl.ds(origin * tr + at, CHUNK)] if src is None else src.at[pl.ds(at, CHUNK)]
        return pltpu.make_async_remote_copy(
            src_ref=source,
            dst_ref=buf.at[pl.ds(place * tr + at, CHUNK)],
            send_sem=send_sem.at[k, kind, ch],
            recv_sem=recv_sem.at[k, min(kind, 3), ch],
            device_id={"row": target},
            device_id_type=pl.DeviceIdType.MESH,
        )

    def send_own(k, ch, src=None):
        send(k, 1, ch, src).start()
        send(k, 0, ch, src).start()

    def forward_partner(k, ch):
        send(k, 1, ch).wait_recv()

        @pl.when(has_ahead)
        def _():
            send(k, 2, ch).start()

            @pl.when(jnp.logical_and(is_near, ch >= nch - DIRECT))
            def _():
                send(k, 4, ch).start()

        @pl.when(jnp.logical_not(is_near))
        def _():
            send(k, 3, ch).start()

    def forward_other(k, ch):
        @pl.when(has_behind)
        def _():
            send(k, 2, ch).wait_recv()

            @pl.when(jnp.logical_and(is_near, ch < nch - DIRECT))
            def _():
                send(k, 3, ch).start()

    def relay(k, step):
        to_partner = step - PARTNER_LAG
        to_other = step - OTHER_LAG

        @pl.when(jnp.logical_and(to_partner >= 0, to_partner < nch))
        def _():
            forward_partner(k, to_partner)

        @pl.when(jnp.logical_and(to_other >= 0, to_other < nch))
        def _():
            forward_other(k, to_other)

    def with_relay(k, work):
        def one(step, _):
            work(step)
            relay(k, step)
            return 0

        def tail(step, _):
            relay(k, step)
            return 0

        def rest(ch, _):
            send(k, 0, ch).wait_recv()

            @pl.when(jnp.logical_or(is_near, has_behind))
            def _():
                send(k, 3, ch).wait_recv()

            return 0

        lax.fori_loop(0, nch, one, 0)
        lax.fori_loop(nch, nch + OTHER_LAG, tail, 0)
        lax.fori_loop(0, nch, rest, 0)

    for ch in range(nch):
        send_own(0, ch, vec)
    for t in range(tr):
        tile_copy(t).start()
    for buf in ext:
        buf[zero_block] = jnp.zeros((tile, width), buf.dtype)

    first_col = (me - REACH) * tr

    for r in range(2 * REACH + 1):
        owner = me - REACH + r
        slot = jnp.where(
            owner == me, OWN,
            jnp.where(owner == sib, SIB, jnp.where(owner == partner, PAR, jnp.where(owner == me - 2 * sign, OTH, EXT))),
        )
        for b in range(tr):
            table[r * tr + b] = slot * tr + b
    table[zero_block] = zero_block

    def place_of(i):
        col = cols[i]
        pos[i] = table[jnp.where(col >= 0, jnp.clip(col - first_col, 0, zero_block), zero_block)]

    share_of = CHUNK * per_row
    part[...] = jnp.zeros_like(part)
    with_relay(0, lambda step: [place_of(step * share_of + j) for j in range(share_of)])
    own_copy.wait()
    for k in range(DEG):
        buf = ext[k]

        def rows_of(ch):
            for r in range(CHUNK):
                t = ch * CHUNK + r
                if k == 0:
                    tile_copy(t).wait()
                lhs = jnp.concatenate([tiles[t * per_row + j] for j in range(per_row)], axis=1)
                rhs = jnp.concatenate([buf[pos[t * per_row + j]] for j in range(per_row)], axis=0)
                acc = jnp.dot(lhs, rhs, preferred_element_type=jnp.float32)
                if k > 0:
                    acc = 2.0 * acc - ext[k - 1][t].astype(jnp.float32)
                y = acc.astype(jnp.bfloat16)
                if k < DEG - 1:
                    ext[k + 1][t] = y
                else:
                    fil[t] = y
                    part[...] += lax.dot_general(y, y, (((0,), (0,)), ((), ())), preferred_element_type=jnp.float32).reshape(part.shape)
            if k < DEG - 1:
                send_own(k + 1, ch)

        if k < DEG - 1:
            with_relay(k + 1, rows_of)
        else:
            def last(ch, _):
                rows_of(ch)
                return 0

            lax.fori_loop(0, nch, last, 0)

    def scatter(d):
        target = lax.rem(me + d, nrow)
        return pltpu.make_async_remote_copy(
            src_ref=part.at[target], dst_ref=rs.at[d], send_sem=g_send.at[d], recv_sem=g_recv.at[d],
            device_id={"row": target}, device_id_type=pl.DeviceIdType.MESH)

    def spread(d):
        target = lax.rem(me + d, nrow)
        return pltpu.make_async_remote_copy(
            src_ref=tot, dst_ref=gath.at[me], send_sem=a_send.at[d], recv_sem=a_recv.at[d],
            device_id={"row": target}, device_id_type=pl.DeviceIdType.MESH)

    for d in range(1, nrow):
        scatter(d).start()

    def rotate(t, _):
        rot[t] = jnp.dot(fil[t], ritz[...], preferred_element_type=jnp.float32).astype(rot.dtype)
        return 0

    lax.fori_loop(0, tr, rotate, 0)
    total = part[me]
    for d in range(1, nrow):
        scatter(d).wait_recv()
        total = total + rs[d]
    total = total * float(nrow * tr * tile) ** (-0.5)
    tot[...] = total
    for d in range(1, nrow):
        spread(d).start()
    gath[me] = total
    for k in range(DEG):
        def drain(ch, _):
            send(k, 0, ch).wait_send()
            send(k, 1, ch).wait_send()

            @pl.when(has_ahead)
            def _():
                send(k, 2, ch).wait_send()

                @pl.when(jnp.logical_and(is_near, ch >= nch - DIRECT))
                def _():
                    send(k, 4, ch).wait_send()

            @pl.when(jnp.logical_or(jnp.logical_not(is_near), jnp.logical_and(has_behind, ch < nch - DIRECT)))
            def _():
                send(k, 3, ch).wait_send()

            return 0

        lax.fori_loop(0, nch, drain, 0)
    for d in range(1, nrow):
        scatter(d).wait_send()
    for d in range(1, nrow):
        spread(d).wait_recv()
        spread(d).wait_send()
    gram[...] = gath[...]


def body(vectors, tiles, tile_cols, ritz):
    rows_here, width = vectors.shape
    tile = tiles.shape[1]
    tr = rows_here // tile
    per_row = tiles.shape[0] // tr
    nrow = lax.axis_size("row")
    nch = tr // CHUNK
    share = (nrow, width // nrow, width)
    vmem = pl.BlockSpec(memory_space=pltpu.VMEM)
    ext = pltpu.VMEM((5 * tr + 1, tile, width), jnp.bfloat16)
    rot, gram = pl.pallas_call(
        functools.partial(kernel, nrow, per_row),
        out_shape=(
            jax.ShapeDtypeStruct((tr, tile, width), jnp.bfloat16),
            jax.ShapeDtypeStruct(share, jnp.float32),
        ),
        in_specs=[
            pl.BlockSpec(memory_space=pl.ANY),
            pl.BlockSpec(memory_space=pl.ANY),
            pl.BlockSpec(memory_space=pltpu.SMEM),
            vmem,
        ],
        out_specs=(vmem, vmem),
        scratch_shapes=[
            ext, ext, ext, ext,
            pltpu.VMEM(tiles.shape, jnp.bfloat16),
            pltpu.SMEM((5 * tr + 1,), jnp.int32),
            pltpu.SMEM((tr * per_row,), jnp.int32),
            pltpu.VMEM((tr, tile, width), jnp.bfloat16),
            pltpu.VMEM(share, jnp.float32),
            pltpu.VMEM(share, jnp.float32),
            pltpu.VMEM(share[1:], jnp.float32),
            pltpu.VMEM(share, jnp.float32),
            pltpu.SemaphoreType.DMA((tr,)),
            pltpu.SemaphoreType.DMA,
            pltpu.SemaphoreType.DMA((DEG, 5, nch)),
            pltpu.SemaphoreType.DMA((DEG, 4, nch)),
            pltpu.SemaphoreType.DMA((nrow,)),
            pltpu.SemaphoreType.DMA((nrow,)),
            pltpu.SemaphoreType.DMA((nrow,)),
            pltpu.SemaphoreType.DMA((nrow,)),
        ],
        compiler_params=pltpu.CompilerParams(
            collective_id=0, has_side_effects=True, vmem_limit_bytes=56 * 2**20
        ),
        cost_estimate=pl.CostEstimate(
            flops=2 * DEG * tiles.size * width, bytes_accessed=2 * tiles.size, transcendentals=0
        ),
    )(vectors.reshape(tr, tile, width), tiles, tile_cols, ritz)
    return rot.reshape(rows_here, width), gram.reshape(width, width)


def solution(mesh):
    return jax.shard_map(
        body,
        mesh=mesh,
        in_specs=(
            P(("parts", "row"), None),
            P(("parts", "row"), None, None),
            P(("parts", "row")),
            P("parts", None),
        ),
        out_specs=(P(("parts", "row"), None), P("parts", None)),
        check_vma=False,
    )
```

```python
import functools

import jax
import jax.numpy as jnp
from jax import lax
from jax.experimental import pallas as pl
from jax.experimental.pallas import tpu as pltpu
from jax.sharding import PartitionSpec as P

REACH = 2
DEG = 4
CHUNK = 1
PARTNER_LAG = 4
OTHER_LAG = 8
DIRECT = 1
OWN, SIB, PAR, OTH, EXT = range(5)


def kernel(nrow, per_row, vec, tiles_hbm, cols, ritz, rot, gram, e0, e1, e2, e3, tiles, table, pos, fil, part, rs, tot, gath,
           tile_sem, own_sem, send_sem, recv_sem, whole_sem, g_send, g_recv, a_send, a_recv):
    ext = (e0, e1, e2, e3)
    tr, tile, width = vec.shape
    nch = tr // CHUNK
    zero_block = 5 * tr
    me = lax.axis_index("row")
    core = lax.rem(me, 2)
    chip = lax.div(me, 2)
    odd = lax.rem(chip, 2)
    sign = 1 - 2 * odd
    near = 1 - odd
    is_near = core == near
    sib = me + 1 - 2 * core
    partner = me + 2 * sign
    ahead = me + 4 * sign
    behind = me - 4 * sign
    far = ahead + 1 - 2 * core
    has_ahead = jnp.logical_and(ahead >= 0, ahead < nrow)
    has_behind = jnp.logical_and(behind >= 0, behind < nrow)

    own_copy = pltpu.make_async_copy(vec, e0.at[pl.ds(0, tr)], own_sem)
    own_copy.start()

    def tile_copy(t):
        rows = pl.ds(t * per_row, per_row)
        return pltpu.make_async_copy(tiles_hbm.at[rows], tiles.at[rows], tile_sem.at[t])

    barrier = pltpu.get_barrier_semaphore()

    def greet(d, _):
        pl.semaphore_signal(barrier, inc=1, device_id={"row": lax.rem(me + d, nrow)}, device_id_type=pl.DeviceIdType.MESH)
        return 0

    lax.fori_loop(1, nrow, greet, 0)
    pl.semaphore_wait(barrier, nrow - 1)

    def send(k, kind, ch, src=None, count=CHUNK):
        buf = ext[k]
        at = ch * CHUNK
        origin, place, target = (
            (OWN, SIB, sib),
            (OWN, PAR, partner),
            (PAR, OTH, ahead),
            (PAR + is_near.astype(jnp.int32), EXT, sib),
            (PAR, EXT, far),
        )[kind]
        source = buf.at[pl.ds(origin * tr + at, count)] if src is None else src.at[pl.ds(at, CHUNK)]
        return pltpu.make_async_remote_copy(
            src_ref=source,
            dst_ref=buf.at[pl.ds(place * tr + at, count)],
            send_sem=send_sem.at[k, kind],
            recv_sem=whole_sem.at[k, min(kind, 3)] if kind in (0, 3, 4) else recv_sem.at[k, kind - 1, ch],
            device_id={"row": target},
            device_id_type=pl.DeviceIdType.MESH,
        )

    def send_own(k, ch, src=None):
        send(k, 1, ch, src).start()
        send(k, 0, ch, src).start()

    def forward_partner(k, ch):
        send(k, 1, ch).wait_recv()

        @pl.when(has_ahead)
        def _():
            send(k, 2, ch).start()

            @pl.when(jnp.logical_and(is_near, ch >= nch - DIRECT))
            def _():
                send(k, 4, ch).start()

        @pl.when(jnp.logical_not(is_near))
        def _():
            send(k, 3, ch).start()

    def forward_other(k, ch):
        @pl.when(has_behind)
        def _():
            send(k, 2, ch).wait_recv()

            @pl.when(jnp.logical_and(is_near, ch < nch - DIRECT))
            def _():
                send(k, 3, ch).start()

    def relay(k, step):
        to_partner = step - PARTNER_LAG
        to_other = step - OTHER_LAG

        @pl.when(jnp.logical_and(to_partner >= 0, to_partner < nch))
        def _():
            forward_partner(k, to_partner)

        @pl.when(jnp.logical_and(to_other >= 0, to_other < nch))
        def _():
            forward_other(k, to_other)

    def with_relay(k, work):
        def one(step, _):
            work(step)
            relay(k, step)
            return 0

        def tail(step, _):
            relay(k, step)
            return 0

        lax.fori_loop(0, nch, one, 0)
        lax.fori_loop(nch, nch + OTHER_LAG, tail, 0)
        send(k, 0, 0, count=tr).wait_recv()

        @pl.when(jnp.logical_or(is_near, has_behind))
        def _():
            send(k, 3, 0, count=tr).wait_recv()

    for ch in range(nch):
        send_own(0, ch, vec)
    for t in range(tr):
        tile_copy(t).start()
    for buf in ext:
        buf[zero_block] = jnp.zeros((tile, width), buf.dtype)

    first_col = (me - REACH) * tr

    for r in range(2 * REACH + 1):
        owner = me - REACH + r
        slot = jnp.where(
            owner == me, OWN,
            jnp.where(owner == sib, SIB, jnp.where(owner == partner, PAR, jnp.where(owner == me - 2 * sign, OTH, EXT))),
        )
        for b in range(tr):
            table[r * tr + b] = slot * tr + b
    table[zero_block] = zero_block

    def place_of(i):
        col = cols[i]
        pos[i] = table[jnp.where(col >= 0, jnp.clip(col - first_col, 0, zero_block), zero_block)]

    share_of = CHUNK * per_row
    part[...] = jnp.zeros_like(part)
    with_relay(0, lambda step: [place_of(step * share_of + j) for j in range(share_of)])
    own_copy.wait()
    for k in range(DEG):
        buf = ext[k]

        def rows_of(ch):
            for r in range(CHUNK):
                t = ch * CHUNK + r
                if k == 0:
                    tile_copy(t).wait()
                lhs = jnp.concatenate([tiles[t * per_row + j] for j in range(per_row)], axis=1)
                rhs = jnp.concatenate([buf[pos[t * per_row + j]] for j in range(per_row)], axis=0)
                acc = jnp.dot(lhs, rhs, preferred_element_type=jnp.float32)
                if k > 0:
                    acc = 2.0 * acc - ext[k - 1][t].astype(jnp.float32)
                y = acc.astype(jnp.bfloat16)
                if k < DEG - 1:
                    ext[k + 1][t] = y
                else:
                    fil[t] = y
                    part[...] += lax.dot_general(y, y, (((0,), (0,)), ((), ())), preferred_element_type=jnp.float32).reshape(part.shape)
            if k < DEG - 1:
                send_own(k + 1, ch)

        if k < DEG - 1:
            with_relay(k + 1, rows_of)
        else:
            def last(pair, _):
                rows_of(2 * pair)
                rows_of(2 * pair + 1)
                return 0

            lax.fori_loop(0, nch // 2, last, 0)

    def scatter(d):
        target = lax.rem(me + d, nrow)
        return pltpu.make_async_remote_copy(
            src_ref=part.at[target], dst_ref=rs.at[d], send_sem=g_send.at[d], recv_sem=g_recv.at[d],
            device_id={"row": target}, device_id_type=pl.DeviceIdType.MESH)

    def spread(d):
        target = lax.rem(me + d, nrow)
        return pltpu.make_async_remote_copy(
            src_ref=tot, dst_ref=gath.at[me], send_sem=a_send.at[d], recv_sem=a_recv.at[d],
            device_id={"row": target}, device_id_type=pl.DeviceIdType.MESH)

    for d in range(1, nrow):
        scatter(d).start()

    def rotate(t, _):
        rot[t] = jnp.dot(fil[t], ritz[...], preferred_element_type=jnp.float32).astype(rot.dtype)
        return 0

    lax.fori_loop(0, tr, rotate, 0)
    total = part[me]
    for d in range(1, nrow):
        scatter(d).wait_recv()
        total = total + rs[d]
    total = total * float(nrow * tr * tile) ** (-0.5)
    tot[...] = total
    for d in range(1, nrow):
        spread(d).start()
    gath[me] = total
    for k in range(DEG):
        send(k, 0, 0, count=tr).wait_send()
        send(k, 1, 0, count=tr).wait_send()

        @pl.when(has_ahead)
        def _():
            send(k, 2, 0, count=tr).wait_send()

            @pl.when(is_near)
            def _():
                send(k, 4, 0, count=DIRECT * CHUNK).wait_send()

        @pl.when(jnp.logical_not(is_near))
        def _():
            send(k, 3, 0, count=tr).wait_send()

        @pl.when(jnp.logical_and(is_near, has_behind))
        def _():
            send(k, 3, 0, count=tr - DIRECT * CHUNK).wait_send()

    for d in range(1, nrow):
        scatter(d).wait_send()
    for d in range(1, nrow):
        spread(d).wait_recv()
        spread(d).wait_send()
    gram[...] = gath[...]


def body(vectors, tiles, tile_cols, ritz):
    rows_here, width = vectors.shape
    tile = tiles.shape[1]
    tr = rows_here // tile
    per_row = tiles.shape[0] // tr
    nrow = lax.axis_size("row")
    nch = tr // CHUNK
    share = (nrow, width // nrow, width)
    vmem = pl.BlockSpec(memory_space=pltpu.VMEM)
    ext = pltpu.VMEM((5 * tr + 1, tile, width), jnp.bfloat16)
    rot, gram = pl.pallas_call(
        functools.partial(kernel, nrow, per_row),
        out_shape=(
            jax.ShapeDtypeStruct((tr, tile, width), jnp.bfloat16),
            jax.ShapeDtypeStruct(share, jnp.float32),
        ),
        in_specs=[
            pl.BlockSpec(memory_space=pl.ANY),
            pl.BlockSpec(memory_space=pl.ANY),
            pl.BlockSpec(memory_space=pltpu.SMEM),
            vmem,
        ],
        out_specs=(vmem, vmem),
        scratch_shapes=[
            ext, ext, ext, ext,
            pltpu.VMEM(tiles.shape, jnp.bfloat16),
            pltpu.SMEM((5 * tr + 1,), jnp.int32),
            pltpu.SMEM((tr * per_row,), jnp.int32),
            pltpu.VMEM((tr, tile, width), jnp.bfloat16),
            pltpu.VMEM(share, jnp.float32),
            pltpu.VMEM(share, jnp.float32),
            pltpu.VMEM(share[1:], jnp.float32),
            pltpu.VMEM(share, jnp.float32),
            pltpu.SemaphoreType.DMA((tr,)),
            pltpu.SemaphoreType.DMA,
            pltpu.SemaphoreType.DMA((DEG, 5)),
            pltpu.SemaphoreType.DMA((DEG, 2, nch)),
            pltpu.SemaphoreType.DMA((DEG, 4)),
            pltpu.SemaphoreType.DMA((nrow,)),
            pltpu.SemaphoreType.DMA((nrow,)),
            pltpu.SemaphoreType.DMA((nrow,)),
            pltpu.SemaphoreType.DMA((nrow,)),
        ],
        compiler_params=pltpu.CompilerParams(
            collective_id=0, has_side_effects=True, vmem_limit_bytes=56 * 2**20
        ),
        cost_estimate=pl.CostEstimate(
            flops=2 * DEG * tiles.size * width, bytes_accessed=2 * tiles.size, transcendentals=0
        ),
    )(vectors.reshape(tr, tile, width), tiles, tile_cols, ritz)
    return rot.reshape(rows_here, width), gram.reshape(width, width)


def solution(mesh):
    return jax.shard_map(
        body,
        mesh=mesh,
        in_specs=(
            P(("parts", "row"), None),
            P(("parts", "row"), None, None),
            P(("parts", "row")),
            P("parts", None),
        ),
        out_specs=(P(("parts", "row"), None), P("parts", None)),
        check_vma=False,
    )
```
